32 devices in a mesh: member: 4 (over y, core), shard: 8 (over z, x).
Axes of the slice: x: 2, y: 2, z: 4, core: 2. Of those that a mesh axis runs over, the one named last changes fastest.
Arguments:
- member_grams: float32 [4, 4096, 4096], P('member', 'shard'), as said below
- member_weights: bfloat16 [4, 4096, 2304], P('member', 'shard'), may hold values from -6 to 6
Outputs:
- merged: float32 [4096, 2304], P('shard', 'member')
The draws below stay inside these ranges and needn't reach their ends.
Inputs may be any that keep to these rules, and one draw needn't show every extreme that they name: `member_grams`: each member's matrix is symmetric positive definite.
All inputs are finite; a program needn't handle non-finite values.
Results may differ from the reference program's by a relative error of at most 0.0032.
Values may be sent and summed in bfloat16 or wider, within the bound.
A program may use at most 128 MiB of HBM per device.

```python
import math
import jax
import jax.numpy as jnp
from jax import lax

K = 4096
OUT = 2304
ITERS = 3
MEMBERS = 4


def draw_member_grams(key, part):
    samples = K // 4
    key_rows = jax.random.fold_in(key, 11)
    key_scales = jax.random.fold_in(key, 23)
    key_coupled = jax.random.fold_in(key, 37)
    key_strength = jax.random.fold_in(key, 41)
    position = jnp.arange(K, dtype=jnp.float32) / K
    strength = jnp.exp(jax.random.uniform(key_strength, (MEMBERS, 1, 2), jnp.float32, math.log(10.0), math.log(80.0)))
    factors = jax.random.normal(key_rows, (MEMBERS, K, samples), jnp.float32)
    spread = jax.random.uniform(key_scales, (MEMBERS, K), jnp.float32, 0.0, math.log(3.3))
    scales = jnp.exp(spread) * jnp.exp(position * math.log(3.0))[None, :]
    coupled = jax.random.normal(key_coupled, (MEMBERS, K, 2), jnp.float32)
    coupled = coupled * jnp.sqrt(strength)
    covariance = jnp.einsum('mks,mjs->mkj', factors, factors, precision=lax.Precision.HIGHEST) / samples
    covariance = covariance + jnp.einsum('mks,mjs->mkj', coupled, coupled, precision=lax.Precision.HIGHEST) / K
    covariance = covariance + 2.0 * jnp.eye(K, dtype=jnp.float32)[None, :, :]
    scaled = covariance * scales[:, :, None] * scales[:, None, :]
    return 0.5 * (scaled + jnp.swapaxes(scaled, 1, 2))


def block_scale(rng, dims, split, low, high):
    factor_of = 1.0
    for dim, shards_of in split:
        steps = jax.random.uniform(jax.random.fold_in(jax.random.fold_in(rng, 6), dim), (shards_of,), jnp.float32, low / len(split), high / len(split))
        factor_of = factor_of * jnp.repeat(jnp.exp(steps), dims[dim] // shards_of).reshape((-1,) + (1,) * (len(dims) - 1 - dim))
    return factor_of


def normal_values(stream_key, extent, scale, limit, pieces=(), held_as=jnp.bfloat16):
    result = jax.random.normal(stream_key, extent, jnp.float32) * scale
    if len(pieces) > 0:
        result = block_scale(stream_key, extent, pieces, -0.22, 0.18) * result
    return jnp.clip(result, min=-limit, max=limit).astype(held_as)


def setup_inputs(seed: int = 0) -> dict:
    key_of = jax.random.split(jax.random.key(seed), 3)
    member_grams = draw_member_grams(jax.random.fold_in(key_of[2], 71), 0)
    member_weights = normal_values(key_of[1], (MEMBERS, K, OUT), 1.0, 6.0, ((0, 4), (1, 8)))
    return dict(member_grams=member_grams, member_weights=member_weights)


shrink = 0.9


def regularize(gram_block, row_offset):
    height = gram_block.shape[-2]
    width = gram_block.shape[-1]
    row_index = lax.broadcasted_iota(jnp.int32, (height, width), 0) + row_offset
    col_index = lax.broadcasted_iota(jnp.int32, (height, width), 1)
    return jnp.where(row_index == col_index, gram_block, shrink * gram_block)


def reference(member_grams, member_weights):
    def accumulate(carry, member):
        gram_matrix, weight_matrix = member
        regular = regularize(gram_matrix, 0)
        gram_low = lax.optimization_barrier(regular.astype(jnp.bfloat16))
        rhs_term = jnp.dot(gram_low.astype(jnp.float32), weight_matrix.astype(jnp.float32),
                           precision=lax.Precision.HIGHEST, preferred_element_type=jnp.float32)
        return (carry[0] + regular, carry[1] + rhs_term), None

    start_carry = (jnp.zeros((K, K), jnp.float32), jnp.zeros((K, OUT), jnp.float32))
    (gram_sum, right_side), unused = lax.scan(accumulate, start_carry, (member_grams, member_weights))
    merged = jnp.zeros((K, OUT), jnp.float32)
    residual = right_side
    direction = right_side
    norm_now = jnp.sum(residual * residual, axis=0)
    for iteration in range(ITERS):
        images = jnp.dot(gram_sum, direction, precision=lax.Precision.HIGHEST,
                         preferred_element_type=jnp.float32)
        step_size = norm_now / jnp.sum(direction * images, axis=0)
        merged = merged + step_size * direction
        residual = residual - step_size * images
        if iteration + 1 < ITERS:
            norm_next = jnp.sum(residual * residual, axis=0)
            direction = residual + (norm_next / norm_now) * direction
            norm_now = norm_next
    return merged
```

```python
import jax
import jax.numpy as jnp
from jax import lax
from jax.sharding import PartitionSpec as P

ITERS = 3


shrink = 0.9


def regularize(gram_block, row_offset):
    height = gram_block.shape[-2]
    width = gram_block.shape[-1]
    row_index = lax.broadcasted_iota(jnp.int32, (height, width), 0) + row_offset
    col_index = lax.broadcasted_iota(jnp.int32, (height, width), 1)
    return jnp.where(row_index == col_index, gram_block, shrink * gram_block)


def norms_of(residual):
    return lax.psum(jnp.sum(residual * residual, axis=0), "shard")


def shards(member_grams, member_weights):
    height = member_grams.shape[1]
    regular = regularize(member_grams, lax.axis_index("shard") * height)
    gram_low = regular.astype(jnp.bfloat16)
    gram_sum = lax.psum(jnp.sum(regular, axis=0), "member")
    partial_rhs = jnp.einsum(
        "mrn,mno->ro",
        gram_low,
        lax.all_gather(member_weights, "shard", axis=1, tiled=True),
        preferred_element_type=jnp.float32,
    )
    right_side = lax.psum_scatter(partial_rhs, "member", scatter_dimension=1, tiled=True)
    gram_used = gram_sum.astype(jnp.bfloat16)
    merged = jnp.zeros_like(right_side)
    residual = right_side
    direction = right_side
    norm_now = norms_of(residual)
    for iteration in range(ITERS):
        images = jnp.dot(
            gram_used,
            lax.all_gather(direction.astype(jnp.bfloat16), "shard", axis=0, tiled=True),
            preferred_element_type=jnp.float32,
        )
        curvature = lax.psum(jnp.sum(direction * images, axis=0), "shard")
        step_size = norm_now / curvature
        merged = merged + step_size * direction
        residual = residual - step_size * images
        if iteration + 1 < ITERS:
            norm_next = norms_of(residual)
            direction = residual + norm_next / norm_now * direction
            norm_now = norm_next
    return merged


def solution(mesh):
    return jax.shard_map(
        shards,
        mesh=mesh,
        in_specs=(P("member", "shard", None), P("member", "shard", None)),
        out_specs=P("shard", "member"),
        check_vma=False,
    )
```

```python
import functools

import jax
import jax.numpy as jnp
from jax import lax
from jax.experimental import pallas as pl
from jax.experimental.pallas import tpu as pltpu
from jax.sharding import PartitionSpec as P

ITERS = 3
MESH = pl.DeviceIdType.MESH


shrink = 0.9


def regularize(gram_block, row_offset):
    height = gram_block.shape[-2]
    width = gram_block.shape[-1]
    row_index = lax.broadcasted_iota(jnp.int32, (height, width), 0) + row_offset
    col_index = lax.broadcasted_iota(jnp.int32, (height, width), 1)
    return jnp.where(row_index == col_index, gram_block, shrink * gram_block)


def greet_all(count):
    me = lax.axis_index("shard")
    barrier = pltpu.get_barrier_semaphore()

    def greet(step, carry):
        pl.semaphore_signal(
            barrier, inc=1, device_id={"shard": lax.rem(me + step, count)}, device_id_type=MESH
        )
        return carry

    lax.fori_loop(1, count, greet, 0)
    pl.semaphore_wait(barrier, count - 1)


def gather_multiply(lines, across, chunks, tile, gram, full, total, recv_sem, line_sem, cross_sem):
    me = lax.axis_index("shard")
    z, x = me // across, lax.rem(me, across)
    height = full.shape[1]
    rows = height // chunks

    def piece(block, k):
        return full.at[block, pl.ds(k * rows, rows)]

    def inside(place):
        return (place >= 0) & (place < lines)

    def line_copy(block, way, t, k, target):
        return pltpu.make_async_remote_copy(
            src_ref=piece(block, k), dst_ref=piece(block, k),
            send_sem=line_sem.at[way, t, k], recv_sem=recv_sem.at[block, k],
            device_id={"shard": target}, device_id_type=MESH,
        )

    def cross_copy(block, way, t, hop, k, target):
        return pltpu.make_async_remote_copy(
            src_ref=piece(block, k), dst_ref=piece(block, k),
            send_sem=cross_sem.at[way, t, hop - 1, k], recv_sem=recv_sem.at[block, k],
            device_id={"shard": target}, device_id_type=MESH,
        )

    def sends(t, act, receive):
        for k in range(chunks):
            for way, sign in enumerate((1, -1)):
                source = z - sign * t
                block = source * across + x
                here = inside(source)
                following = z + sign
                if receive:
                    @pl.when(here & (t > 0))
                    def _():
                        line_copy(block, way, t, k, me).wait_recv()

                @pl.when(here & inside(following))
                def _():
                    act(line_copy(block, way, t, k, following * across + x))

                @pl.when(here & ((t > 0) | (sign > 0)))
                def _():
                    for hop in range(1, across):
                        act(cross_copy(block, way, t, hop, k, z * across + lax.rem(x + hop, across)))

    def multiply(t):
        for way, sign in enumerate((1, -1)):
            source = z - sign * t

            @pl.when(inside(source) & ((t > 0) | (sign > 0)))
            def _():
                def one(hop, carry):
                    block = source * across + lax.rem(x + hop, across)

                    @pl.when(hop > 0)
                    def _():
                        for k in range(chunks):
                            line_copy(block, way, t, k, me).wait_recv()

                    left = gram[:, pl.ds(pl.multiple_of(block * height, height), height)]
                    if tile == total.shape[1]:
                        total[...] += jnp.dot(left, full[block], preferred_element_type=jnp.float32)
                    else:
                        def columns(j, inner):
                            at = pl.ds(pl.multiple_of(j * tile, tile), tile)
                            total[:, at] += jnp.dot(
                                left, full[block, :, at], preferred_element_type=jnp.float32
                            )
                            return inner

                        lax.fori_loop(0, total.shape[1] // tile, columns, 0)
                    return carry

                lax.fori_loop(0, across, one, 0)

    def step(t, carry):
        sends(t, lambda copy: copy.start(), True)

        @pl.when(t > 0)
        def _():
            multiply(t - 1)

        return carry

    lax.fori_loop(0, lines, step, 0)
    multiply(jnp.int32(lines - 1))

    def finish(t, carry):
        sends(t, lambda copy: copy.wait_send(), False)
        return carry

    lax.fori_loop(0, lines, finish, 0)


def weigh_kernel(lines, across, chunks, tile, gram, weights, total, full, recv_sem, line_sem, cross_sem):
    me = lax.axis_index("shard")
    full[me] = weights[...]
    total[...] = jnp.zeros_like(total)
    greet_all(lines * across)
    gather_multiply(lines, across, chunks, tile, gram, full, total, recv_sem, line_sem, cross_sem)


def solve_kernel(lines, across, chunks, gram, right_side, merged, full, residual, direction, image,
                 product, sums, recv_sem, line_sem, cross_sem, sums_send, sums_recv):
    me = lax.axis_index("shard")
    count = lines * across
    width = residual.shape[1]

    def sum_copy(which, slot, step, target):
        return pltpu.make_async_remote_copy(
            src_ref=sums.at[which, slot], dst_ref=sums.at[which, slot],
            send_sem=sums_send.at[which, step], recv_sem=sums_recv.at[which, slot],
            device_id={"shard": target}, device_id_type=MESH,
        )

    def sum_start(which, values):
        sums[which, me] = jnp.sum(values.reshape(-1, 8, width), axis=0)

        def send(step, carry):
            sum_copy(which, me, step, lax.rem(me + step, count)).start()
            return carry

        lax.fori_loop(1, count, send, 0)

    def sum_finish(which):
        def receive(step, carry):
            sum_copy(which, lax.rem(me + step, count), step, me).wait_recv()
            return carry

        lax.fori_loop(1, count, receive, 0)
        result = jnp.sum(jnp.sum(sums[which], axis=0), axis=0, keepdims=True)

        def sent(step, carry):
            sum_copy(which, me, step, lax.rem(me + step, count)).wait_send()
            return carry

        lax.fori_loop(1, count, sent, 0)
        return result

    greet_all(count)
    residual[...] = right_side[...]
    merged[...] = jnp.zeros_like(merged)
    norm_now = None
    for iteration in range(ITERS):
        now = residual[...]
        full[me] = now.astype(jnp.bfloat16)
        sum_start(2 * iteration, now * now)
        product[...] = jnp.zeros_like(product)
        gather_multiply(lines, across, chunks, width, gram, full, product, recv_sem, line_sem, cross_sem)
        norm_next = sum_finish(2 * iteration)
        if iteration == 0:
            direction[...] = residual[...]
            image[...] = product[...]
        else:
            ratio = norm_next / norm_now
            direction[...] = residual[...] + ratio * direction[...]
            image[...] = product[...] + ratio * image[...]
        norm_now = norm_next
        sum_start(2 * iteration + 1, direction[...] * image[...])
        step_size = norm_now / sum_finish(2 * iteration + 1)
        merged[...] += step_size * direction[...]
        if iteration + 1 < ITERS:
            residual[...] -= step_size * image[...]


def gather_scratch(lines, across, chunks):
    return [
        pltpu.SemaphoreType.DMA((lines * across, chunks)),
        pltpu.SemaphoreType.DMA((2, lines, chunks)),
        pltpu.SemaphoreType.DMA((2, lines, max(across - 1, 1), chunks)),
    ]


def widest(width):
    for tile in range(width // 128 * 128, 0, -128):
        if tile <= 768 and width % tile == 0:
            return tile
    return width


def shards(lines, across, member_grams, member_weights):
    height = member_grams.shape[1]
    features = member_weights.shape[2]
    count = lines * across
    regular = regularize(member_grams[0], lax.axis_index("shard") * height)
    gram_low = regular.astype(jnp.bfloat16)
    gram_sum = lax.psum(regular, "member").astype(jnp.bfloat16)
    vmem = pl.BlockSpec(memory_space=pltpu.VMEM)
    partial_rhs = pl.pallas_call(
        functools.partial(weigh_kernel, lines, across, 4, widest(features)),
        out_shape=jax.ShapeDtypeStruct((height, features), jnp.float32),
        in_specs=[vmem, vmem],
        out_specs=vmem,
        scratch_shapes=[pltpu.VMEM((count, height, features), jnp.bfloat16)]
        + gather_scratch(lines, across, 4),
        compiler_params=pltpu.CompilerParams(
            collective_id=0, has_side_effects=True, vmem_limit_bytes=48 << 20
        ),
    )(gram_low, member_weights[0])
    right_side = lax.psum_scatter(partial_rhs, "member", scatter_dimension=1, tiled=True)
    width = right_side.shape[1]
    state = pltpu.VMEM((height, width), jnp.float32)
    return pl.pallas_call(
        functools.partial(solve_kernel, lines, across, 2),
        out_shape=jax.ShapeDtypeStruct((height, width), jnp.float32),
        in_specs=[vmem, vmem],
        out_specs=vmem,
        scratch_shapes=[pltpu.VMEM((count, height, width), jnp.bfloat16)]
        + [state] * 4
        + [pltpu.VMEM((2 * ITERS, count, 8, width), jnp.float32)]
        + gather_scratch(lines, across, 2)
        + [pltpu.SemaphoreType.DMA((2 * ITERS, count)), pltpu.SemaphoreType.DMA((2 * ITERS, count))],
        compiler_params=pltpu.CompilerParams(
            collective_id=1, has_side_effects=True, vmem_limit_bytes=40 << 20
        ),
    )(gram_sum, right_side)


def solution(mesh):
    count = mesh.shape["shard"]
    places = {getattr(device, "coords", (0,))[0] for device in mesh.devices.flat}
    across = len(places) if count % len(places) == 0 else 1
    return jax.shard_map(
        functools.partial(shards, count // across, across),
        mesh=mesh,
        in_specs=(P("member", "shard", None), P("member", "shard", None)),
        out_specs=P("shard", "member"),
        check_vma=False,
    )
```

```python
import functools

import jax
import jax.numpy as jnp
from jax import lax
from jax.experimental import pallas as pl
from jax.experimental.pallas import tpu as pltpu
from jax.sharding import PartitionSpec as P

ITERS = 3
MESH = pl.DeviceIdType.MESH


shrink = 0.9


def regularize(gram_block, row_offset):
    height = gram_block.shape[-2]
    width = gram_block.shape[-1]
    row_index = lax.broadcasted_iota(jnp.int32, (height, width), 0) + row_offset
    col_index = lax.broadcasted_iota(jnp.int32, (height, width), 1)
    return jnp.where(row_index == col_index, gram_block, shrink * gram_block)


def greet_all(count):
    me = lax.axis_index("shard")
    barrier = pltpu.get_barrier_semaphore()

    def greet(step, carry):
        pl.semaphore_signal(
            barrier, inc=1, device_id={"shard": lax.rem(me + step, count)}, device_id_type=MESH
        )
        return carry

    lax.fori_loop(1, count, greet, 0)
    pl.semaphore_wait(barrier, count - 1)


def gather_multiply(lines, across, chunks, tile, gram, full, total, recv_sem, line_sem, cross_sem):
    me = lax.axis_index("shard")
    z, x = me // across, lax.rem(me, across)
    height = full.shape[1]
    rows = height // chunks

    def piece(block, k):
        return full.at[block, pl.ds(k * rows, rows)]

    def inside(place):
        return (place >= 0) & (place < lines)

    def line_copy(block, way, t, k, target):
        return pltpu.make_async_remote_copy(
            src_ref=piece(block, k), dst_ref=piece(block, k),
            send_sem=line_sem.at[way, t, k], recv_sem=recv_sem.at[block, k],
            device_id={"shard": target}, device_id_type=MESH,
        )

    def cross_copy(block, way, t, hop, k, target):
        return pltpu.make_async_remote_copy(
            src_ref=piece(block, k), dst_ref=piece(block, k),
            send_sem=cross_sem.at[way, t, hop - 1, k], recv_sem=recv_sem.at[block, k],
            device_id={"shard": target}, device_id_type=MESH,
        )

    def sends(t, act, receive):
        for k in range(chunks):
            for way, sign in enumerate((1, -1)):
                source = z - sign * t
                block = source * across + x
                here = inside(source)
                following = z + sign
                if receive:
                    @pl.when(here & (t > 0))
                    def _():
                        line_copy(block, way, t, k, me).wait_recv()

                @pl.when(here & inside(following))
                def _():
                    act(line_copy(block, way, t, k, following * across + x))

                @pl.when(here & ((t > 0) | (sign > 0)))
                def _():
                    for hop in range(1, across):
                        act(cross_copy(block, way, t, hop, k, z * across + lax.rem(x + hop, across)))

    def multiply(t):
        for way, sign in enumerate((1, -1)):
            source = z - sign * t

            @pl.when(inside(source) & ((t > 0) | (sign > 0)))
            def _():
                def one(hop, carry):
                    block = source * across + lax.rem(x + hop, across)

                    @pl.when(hop > 0)
                    def _():
                        for k in range(chunks):
                            line_copy(block, way, t, k, me).wait_recv()

                    left = gram[:, pl.ds(pl.multiple_of(block * height, height), height)]
                    if tile == total.shape[1]:
                        total[...] += jnp.dot(left, full[block], preferred_element_type=jnp.float32)
                    else:
                        def columns(j, inner):
                            at = pl.ds(pl.multiple_of(j * tile, tile), tile)
                            total[:, at] += jnp.dot(
                                left, full[block, :, at], preferred_element_type=jnp.float32
                            )
                            return inner

                        lax.fori_loop(0, total.shape[1] // tile, columns, 0)
                    return carry

                lax.fori_loop(0, across, one, 0)

    def step(t, carry):
        sends(t, lambda copy: copy.start(), True)

        @pl.when(t > 0)
        def _():
            multiply(t - 1)

        return carry

    lax.fori_loop(0, lines, step, 0)
    multiply(jnp.int32(lines - 1))

    def finish(t, carry):
        sends(t, lambda copy: copy.wait_send(), False)
        return carry

    lax.fori_loop(0, lines, finish, 0)


def weigh_kernel(lines, across, chunks, tile, gram, weights, out, full, total, recv_sem, line_sem, cross_sem):
    me = lax.axis_index("shard")
    full[me] = weights[...]
    total[...] = jnp.zeros_like(total)
    greet_all(lines * across)
    gather_multiply(lines, across, chunks, tile, gram, full, total, recv_sem, line_sem, cross_sem)
    width = out.shape[2]
    for member in range(out.shape[0]):
        out[member] = total[:, member * width:(member + 1) * width]


def solve_kernel(lines, across, chunks, gram_sum, right_side, merged, gram, full, residual, direction, image,
                 product, sums, recv_sem, line_sem, cross_sem, sums_send, sums_recv):
    me = lax.axis_index("shard")
    count = lines * across
    width = residual.shape[1]

    def sum_copy(which, slot, step, target):
        return pltpu.make_async_remote_copy(
            src_ref=sums.at[which, slot], dst_ref=sums.at[which, slot],
            send_sem=sums_send.at[which, step], recv_sem=sums_recv.at[which, slot],
            device_id={"shard": target}, device_id_type=MESH,
        )

    def sum_start(which, values):
        sums[which, me] = jnp.sum(values.reshape(-1, 8, width), axis=0)

        def send(step, carry):
            sum_copy(which, me, step, lax.rem(me + step, count)).start()
            return carry

        lax.fori_loop(1, count, send, 0)

    def sum_finish(which):
        def receive(step, carry):
            sum_copy(which, lax.rem(me + step, count), step, me).wait_recv()
            return carry

        lax.fori_loop(1, count, receive, 0)
        result = jnp.sum(jnp.sum(sums[which], axis=0), axis=0, keepdims=True)

        def sent(step, carry):
            sum_copy(which, me, step, lax.rem(me + step, count)).wait_send()
            return carry

        lax.fori_loop(1, count, sent, 0)
        return result

    greet_all(count)
    gram[...] = gram_sum[...].astype(jnp.bfloat16)
    residual[...] = right_side[...]
    merged[...] = jnp.zeros_like(merged)
    norm_now = None
    for iteration in range(ITERS):
        now = residual[...]
        full[me] = now.astype(jnp.bfloat16)
        sum_start(2 * iteration, now * now)
        product[...] = jnp.zeros_like(product)
        gather_multiply(lines, across, chunks, width, gram, full, product, recv_sem, line_sem, cross_sem)
        norm_next = sum_finish(2 * iteration)
        if iteration == 0:
            direction[...] = residual[...]
            image[...] = product[...]
        else:
            ratio = norm_next / norm_now
            direction[...] = residual[...] + ratio * direction[...]
            image[...] = product[...] + ratio * image[...]
        norm_now = norm_next
        sum_start(2 * iteration + 1, direction[...] * image[...])
        step_size = norm_now / sum_finish(2 * iteration + 1)
        merged[...] += step_size * direction[...]
        if iteration + 1 < ITERS:
            residual[...] -= step_size * image[...]


def gather_scratch(lines, across, chunks):
    return [
        pltpu.SemaphoreType.DMA((lines * across, chunks)),
        pltpu.SemaphoreType.DMA((2, lines, chunks)),
        pltpu.SemaphoreType.DMA((2, lines, max(across - 1, 1), chunks)),
    ]


def widest(width):
    for tile in range(width // 128 * 128, 0, -128):
        if tile <= 768 and width % tile == 0:
            return tile
    return width


def shards(lines, across, members, member_grams, member_weights):
    height = member_grams.shape[1]
    features = member_weights.shape[2]
    count = lines * across
    regular = regularize(member_grams[0], lax.axis_index("shard") * height)
    gram_low = regular.astype(jnp.bfloat16)
    gram_sum = lax.psum(regular, "member")
    vmem = pl.BlockSpec(memory_space=pltpu.VMEM)
    partial_rhs = pl.pallas_call(
        functools.partial(weigh_kernel, lines, across, 4, widest(features)),
        out_shape=jax.ShapeDtypeStruct((members, height, features // members), jnp.float32),
        in_specs=[vmem, vmem],
        out_specs=vmem,
        scratch_shapes=[
            pltpu.VMEM((count, height, features), jnp.bfloat16),
            pltpu.VMEM((height, features), jnp.float32),
        ]
        + gather_scratch(lines, across, 4),
        compiler_params=pltpu.CompilerParams(
            collective_id=0, has_side_effects=True, vmem_limit_bytes=48 << 20
        ),
        cost_estimate=pl.CostEstimate(
            flops=16 * count * height * height * features,
            bytes_accessed=8 * count * height * features,
            transcendentals=0,
        ),
    )(gram_low, member_weights[0])
    right_side = lax.psum_scatter(partial_rhs, "member", scatter_dimension=0, tiled=False)
    width = right_side.shape[1]
    state = pltpu.VMEM((height, width), jnp.float32)
    return pl.pallas_call(
        functools.partial(solve_kernel, lines, across, 2),
        out_shape=jax.ShapeDtypeStruct((height, width), jnp.float32),
        in_specs=[vmem, vmem],
        out_specs=vmem,
        scratch_shapes=[
            pltpu.VMEM((height, count * height), jnp.bfloat16),
            pltpu.VMEM((count, height, width), jnp.bfloat16),
        ]
        + [state] * 4
        + [pltpu.VMEM((2 * ITERS, count, 8, width), jnp.float32)]
        + gather_scratch(lines, across, 2)
        + [pltpu.SemaphoreType.DMA((2 * ITERS, count)), pltpu.SemaphoreType.DMA((2 * ITERS, count))],
        compiler_params=pltpu.CompilerParams(
            collective_id=1, has_side_effects=True, vmem_limit_bytes=40 << 20
        ),
    )(gram_sum, right_side)


def solution(mesh):
    count = mesh.shape["shard"]
    places = {getattr(device, "coords", (0,))[0] for device in mesh.devices.flat}
    across = len(places) if count % len(places) == 0 else 1
    return jax.shard_map(
        functools.partial(shards, count // across, across, mesh.shape["member"]),
        mesh=mesh,
        in_specs=(P("member", "shard", None), P("member", "shard", None)),
        out_specs=P("shard", "member"),
        check_vma=False,
    )
```
